512 devices in a mesh: ctx: 128 (over z, x, core), kvh: 4 (over y).
Axes of the slice: x: 4, y: 4, z: 16, core: 2. Of those that a mesh axis runs over, the one named last changes fastest.
Arguments:
- queries: bfloat16 [32768, 4, 1024], P('ctx', 'kvh'), may hold values from -8 to 8
- keys: bfloat16 [32768, 1024], P('ctx', 'kvh'), may hold values from -8 to 8
- values: bfloat16 [32768, 1024], P('ctx', 'kvh'), may hold values from -6 to 6
- out_grad: bfloat16 [32768, 4, 1024], P('ctx', 'kvh'), may hold values from -6 to 6
- doc_lengths: int32 [64], replicated, may hold values from 1 to 768, 32768 in all
Outputs:
- query_grad: bfloat16 [32768, 4, 1024], P('ctx', 'kvh')
- key_grad: bfloat16 [32768, 1024], P('ctx', 'kvh')
- value_grad: bfloat16 [32768, 1024], P('ctx', 'kvh')
The draws below stay inside these ranges and needn't reach their ends.
Inputs may be any that keep to these rules, and one draw needn't show every extreme that they name: `doc_lengths`: 64 documents in order that fill all 32768 positions; the longest has exactly 768 positions.
All inputs are finite; a program needn't handle non-finite values.
Results may differ from the reference program's by a relative error of at most 0.028.
Values may be sent and summed in bfloat16 or wider, within the bound.
No kernel may reach another device: no remote copies, remote signals or barrier semaphores. Data moves between devices by JAX's collectives and lax.ppermute only.
A program may use at most 64 MiB of HBM per device.

```python
import math
import jax
import jax.numpy as jnp
import numpy as np
from jax import lax

KVH = 8
HD = 128
REP = 4
SEQ = 32768
MOST = 768
DOCS = 64


def draw_queries(key, part):
    key = jax.random.fold_in(key, 7)
    base = jax.random.truncated_normal(key, -6.0, 6.0, (SEQ, REP, KVH * HD), jnp.float32)
    return base.astype(jnp.bfloat16)


def draw_keys(key, part):
    key = jax.random.fold_in(key, 13)
    base = jax.random.truncated_normal(key, -6.0, 6.0, (SEQ, KVH * HD), jnp.float32)
    return base.astype(jnp.bfloat16)


def steps_of(rng, shape, shards, least, top_value):
    factor_of = 1.0
    for axis_at, shards_of in shards:
        heights = jax.random.uniform(jax.random.fold_in(jax.random.fold_in(rng, 6), axis_at), (shards_of,), jnp.float32, least / len(shards), top_value / len(shards))
        factor_of = factor_of * jnp.repeat(jnp.exp(heights), shape[axis_at] // shards_of).reshape((-1,) + (1,) * (len(shape) - 1 - axis_at))
    return factor_of


def split_up(amount, total, reach, slope):
    weights = [(1 << 20) // math.isqrt(standing ** slope) + 1 for standing in range(2, amount + 1)]
    spare, holding = total - reach - (amount - 1), [1] * (amount - 1)
    while spare > 0:
        free = [i for i in range(amount - 1) if holding[i] < reach]
        pool, left = sum([weights[i] for i in free]), spare
        for i in free:
            addition = min(reach - holding[i], max(1, left * weights[i] // pool), spare)
            holding[i] = holding[i] + addition
            spare = spare - addition
    return np.array([reach] + holding)


def uneven(rng, amount, total, limit, lean):
    if amount == 2:
        one = jax.random.randint(rng, (), max(1, total - limit), min(limit, total - 1) + 1)
        return jnp.stack([one, total - one])
    tallies = jnp.asarray(split_up(amount, total, limit, lean), jnp.int32)
    couples = (amount - 1) // 2
    donor, sink = tallies[1:1 + 2 * couples:2], tallies[2:2 + 2 * couples:2]
    room = jnp.minimum(donor - 1, limit - sink)
    shifted = jax.random.randint(jax.random.fold_in(rng, 1), (couples,), 0, 1 << 20) % (room + 1)
    tallies = tallies.at[1:1 + 2 * couples:2].set(donor - shifted).at[2:2 + 2 * couples:2].set(sink + shifted)
    return tallies[jax.random.permutation(jax.random.fold_in(rng, 2), amount)]


def normal_values(rng, extent, spread, bound, cuts=(), kind=jnp.bfloat16):
    drawn = spread * jax.random.normal(rng, extent, jnp.float32)
    if cuts:
        drawn = drawn * steps_of(rng, extent, cuts, -0.22, 0.18)
    return jnp.clip(drawn, -bound, bound).astype(kind)


def setup_inputs(seed: int = 0) -> dict:
    key_list = jax.random.split(jax.random.key(seed), 6)
    return {
        "queries": draw_queries(jax.random.fold_in(key_list[5], 71), 0),
        "keys": draw_keys(jax.random.fold_in(key_list[5], 71), 0),
        "values": normal_values(key_list[2], (SEQ, KVH * HD), 1.0, 6.0, ((0, 128), (1, 4))),
        "out_grad": normal_values(key_list[3], (SEQ, REP, KVH * HD), 1.0, 6.0, ((0, 128), (1, 4))),
        "doc_lengths": uneven(key_list[4], DOCS, SEQ, MOST, 1).astype(jnp.int32),
    }


def rounded(array):
    return lax.optimization_barrier(array.astype(jnp.bfloat16)).astype(jnp.float32)

def doc_index(positions, ends):
    return lax.optimization_barrier(jnp.sum((positions[:, None] >= ends[None, :]).astype(jnp.int32), axis=1)).astype(jnp.int32)

def reference(queries, keys, values, out_grad, doc_lengths):
    ends = jnp.cumsum(doc_lengths).astype(jnp.int32)
    segment = doc_index(jnp.arange(SEQ, dtype=jnp.int32), ends)
    margin = MOST
    block = math.gcd(SEQ, 256)
    span = margin + block
    scale = 1.0 / math.sqrt(HD)
    key_pad = jnp.concatenate([jnp.zeros((margin, KVH, HD), jnp.float32), keys.reshape(SEQ, KVH, HD).astype(jnp.float32)], axis=0)
    value_pad = jnp.concatenate([jnp.zeros((margin, KVH, HD), jnp.float32), values.reshape(SEQ, KVH, HD).astype(jnp.float32)], axis=0)
    seg_pad = jnp.concatenate([jnp.full((margin,), -1, jnp.int32), segment])
    query_all = queries.reshape(SEQ, REP, KVH, HD).astype(jnp.float32)
    grad_all = out_grad.reshape(SEQ, REP, KVH, HD).astype(jnp.float32)

    def one_block(carry, index):
        key_acc, value_acc = carry
        start = (index * block).astype(jnp.int32)
        query_blk = lax.dynamic_slice_in_dim(query_all, start, block, 0)
        grad_blk = lax.dynamic_slice_in_dim(grad_all, start, block, 0)
        key_blk = lax.dynamic_slice_in_dim(key_pad, start, span, 0)
        value_blk = lax.dynamic_slice_in_dim(value_pad, start, span, 0)
        query_pos = start + jnp.arange(block, dtype=jnp.int32)
        key_pos = start - margin + jnp.arange(span, dtype=jnp.int32)
        query_seg = lax.dynamic_slice_in_dim(segment, start, block, 0)
        key_seg = lax.dynamic_slice_in_dim(seg_pad, start, span, 0)
        allowed = (query_seg[:, None] == key_seg[None, :]) & (key_pos[None, :] <= query_pos[:, None])
        scores = jnp.einsum('qrgd,kgd->rgqk', query_blk, key_blk) * scale
        scores = jnp.where(allowed, scores, -1e+30)
        top = lax.optimization_barrier(jnp.max(scores, axis=-1, keepdims=True))
        total = lax.optimization_barrier(jnp.sum(jnp.where(allowed, jnp.exp(scores - top), 0.0), axis=-1, keepdims=True))
        log_total = top + jnp.log(total)
        weights = jnp.where(allowed, jnp.exp(scores - log_total), 0.0)
        weights_low = rounded(weights)
        output = rounded(jnp.einsum('rgqk,kgd->qrgd', weights_low, value_blk))
        delta = jnp.einsum('qrgd,qrgd->rgq', grad_blk, output)
        grad_weights = jnp.einsum('qrgd,kgd->rgqk', grad_blk, value_blk)
        grad_scores = rounded(weights * (grad_weights - delta[..., None]))
        grad_query = jnp.einsum('rgqk,kgd->qrgd', grad_scores, key_blk) * scale
        grad_key = jnp.einsum('rgqk,qrgd->kgd', grad_scores, query_blk) * scale
        grad_value = jnp.einsum('rgqk,qrgd->kgd', weights_low, grad_blk)
        key_acc = lax.dynamic_update_slice_in_dim(key_acc, lax.dynamic_slice_in_dim(key_acc, start, span, 0) + grad_key, start, 0)
        value_acc = lax.dynamic_update_slice_in_dim(value_acc, lax.dynamic_slice_in_dim(value_acc, start, span, 0) + grad_value, start, 0)
        return ((key_acc, value_acc), grad_query.astype(jnp.bfloat16))
    zeros = jnp.zeros((margin + SEQ, KVH, HD), jnp.float32)
    (key_acc, value_acc), grad_blocks = lax.scan(one_block, (zeros, zeros), jnp.arange(SEQ // block, dtype=jnp.int32))
    query_grad = grad_blocks.reshape(SEQ, REP, KVH * HD)
    key_grad = key_acc[margin:].reshape(SEQ, KVH * HD).astype(jnp.bfloat16)
    value_grad = value_acc[margin:].reshape(SEQ, KVH * HD).astype(jnp.bfloat16)
    return (query_grad, key_grad, value_grad)
```

```python
import math

import jax
import jax.numpy as jnp
from jax import lax
from jax.experimental import pallas as pl
from jax.experimental.pallas import tpu as pltpu
from jax.sharding import PartitionSpec as P

HD = 128
ROWS = 256
BACK = 3
SPAN = (BACK + 1) * ROWS
REPS = 4
HEADS = 2
SCALE = 1.0 / math.sqrt(HD)
LOG2E = 1.0 / math.log(2.0)

NT = (((1,), (1,)), ((), ()))
NN = (((1,), (0,)), ((), ()))
TN = (((0,), (0,)), ((), ()))


def dot(a, b, dims):
    return lax.dot_general(a, b, dims, preferred_element_type=jnp.float32)


def shifted(value, by):
    length = lax.axis_size("ctx")
    pairs = [(i, i + by) for i in range(length) if 0 <= i + by < length]
    return lax.ppermute(value, "ctx", pairs)


def pack_body(q_ref, g_ref, k_ref, v_ref, qg_ref, kv_ref):
    for y in range(REPS):
        cols = pl.ds(y * 256, 256)
        qg_ref[y, 0] = q_ref[0, :, cols]
        qg_ref[y, 1] = g_ref[0, :, cols]
    kv_ref[0] = k_ref[...]
    kv_ref[1] = v_ref[...]


def attend_body(
    len_ref, qg_ref, b0, b1, b2, b3, dq_ref, far0, far1, far2, own,
    s_ref, d_ref, w_ref, t_ref,
):
    blocks = (b0, b1, b2, b3)
    outs = (far0, far1, far2, own)
    docs = len_ref.shape[1]
    origin = lax.axis_index("ctx") * ROWS - BACK * ROWS
    at = lax.broadcasted_iota(jnp.int32, (docs, docs), 0)
    of = lax.broadcasted_iota(jnp.int32, (docs, docs), 1)
    ends = jnp.sum(jnp.where(of <= at, len_ref[...], 0), axis=1, keepdims=True)
    pos = origin + BACK * ROWS + lax.broadcasted_iota(jnp.int32, (docs, ROWS), 1)
    first = jnp.max(jnp.where(ends <= pos, ends, 0), axis=0, keepdims=True) - origin
    key_at = lax.broadcasted_iota(jnp.int32, (ROWS, ROWS), 0)
    row_at = lax.broadcasted_iota(jnp.int32, (ROWS, ROWS), 1)

    for h in range(HEADS):
        cols = pl.ds(h * HD, HD)
        for r in range(REPS):
            rows = pl.ds(r * ROWS, ROWS)
            query = qg_ref[r, 0, :, cols]
            grad = qg_ref[r, 1, :, cols]
            top = None
            for b in range(BACK + 1):
                s = dot(blocks[b][0, :, cols], query, NT)
                allowed = key_at >= first - b * ROWS
                if b == BACK:
                    allowed = allowed & (key_at <= row_at)
                s = jnp.where(allowed, s, -1e30)
                s_ref[r, pl.ds(b * ROWS, ROWS), :] = s
                part = jnp.max(s, axis=0, keepdims=True)
                top = part if top is None else jnp.maximum(top, part)
            total = jnp.zeros((1, ROWS), jnp.float32)
            inner = jnp.zeros((1, ROWS), jnp.float32)
            for b in range(BACK + 1):
                keys = pl.ds(b * ROWS, ROWS)
                p = jnp.exp2((s_ref[r, keys, :] - top) * (SCALE * LOG2E))
                d = dot(blocks[b][1, :, cols], grad, NT)
                total = total + jnp.sum(p, axis=0, keepdims=True)
                inner = inner + jnp.sum(p * d, axis=0, keepdims=True)
                s_ref[r, keys, :] = p
                d_ref[r, keys, :] = d
            norm = 1.0 / total
            delta = inner * norm
            for b in range(BACK + 1):
                keys = pl.ds(b * ROWS, ROWS)
                w = s_ref[r, keys, :] * norm
                w_ref[keys, rows] = w.astype(jnp.bfloat16)
                t_ref[keys, rows] = (w * (d_ref[r, keys, :] - delta)).astype(jnp.bfloat16)
            dq = None
            for b in range(BACK + 1):
                part = dot(blocks[b][0, :, cols], t_ref[pl.ds(b * ROWS, ROWS), rows], TN)
                dq = part if dq is None else dq + part
            dq_ref[r, :, cols] = (dq * SCALE).T.astype(jnp.bfloat16)
        queries = jnp.concatenate([qg_ref[r, 0, :, cols] for r in range(REPS)], axis=0)
        grads = jnp.concatenate([qg_ref[r, 1, :, cols] for r in range(REPS)], axis=0)
        for b in range(BACK + 1):
            keys = pl.ds(b * ROWS, ROWS)
            dk = dot(t_ref[keys, :], queries, NN) * SCALE
            dv = dot(w_ref[keys, :], grads, NN)
            outs[b][0, :, cols] = dk.astype(outs[b].dtype)
            outs[b][1, :, cols] = dv.astype(outs[b].dtype)


def finish_body(own, n1, n2, n3, dq_ref, k_ref, v_ref, q_ref):
    total = own[...] + (n1[...].astype(jnp.float32) + n2[...].astype(jnp.float32) + n3[...].astype(jnp.float32))
    k_ref[...] = total[0].astype(jnp.bfloat16)
    v_ref[...] = total[1].astype(jnp.bfloat16)
    for y in range(REPS):
        q_ref[0, :, pl.ds(y * 256, 256)] = dq_ref[y]


VM = pl.BlockSpec(memory_space=pltpu.VMEM)


def call(body, n_in, out_shape, scratch=(), flops=0, bytes_=1 << 20, vmem=48 << 20):
    return pl.pallas_call(
        body,
        out_shape=out_shape,
        in_specs=[VM] * n_in,
        out_specs=jax.tree.map(lambda _: VM, out_shape),
        scratch_shapes=list(scratch),
        compiler_params=pltpu.CompilerParams(vmem_limit_bytes=vmem),
        cost_estimate=pl.CostEstimate(flops=flops, bytes_accessed=bytes_, transcendentals=0),
    )


def shape(dims, dtype=jnp.bfloat16):
    return jax.ShapeDtypeStruct(dims, dtype)


def per_device(queries, keys, values, out_grad, doc_lengths):
    q = jnp.transpose(queries, (1, 0, 2))
    g = jnp.transpose(out_grad, (1, 0, 2))
    qg, kv = call(pack_body, 4, (shape((REPS, 2, ROWS, 256)), shape((2, ROWS, 256))))(q, g, keys, values)
    qg = lax.all_to_all(qg, "kvh", 0, 0, tiled=True)
    back = [shifted(kv, by) for by in (3, 2, 1)]
    block = (2, ROWS, 256)
    dq, far3, far2, far1, own = call(
        attend_body,
        6,
        (shape((REPS, ROWS, 256)), shape(block), shape(block), shape(block), shape(block, jnp.float32)),
        scratch=(
            pltpu.VMEM((REPS, SPAN, ROWS), jnp.float32),
            pltpu.VMEM((REPS, SPAN, ROWS), jnp.float32),
            pltpu.VMEM((SPAN, REPS * ROWS), jnp.bfloat16),
            pltpu.VMEM((SPAN, REPS * ROWS), jnp.bfloat16),
        ),
        flops=3 << 30,
    )(doc_lengths.reshape(1, -1), qg, *back, kv)
    n3, n2, n1 = shifted(far3, -3), shifted(far2, -2), shifted(far1, -1)
    dq = lax.all_to_all(dq, "kvh", 0, 0, tiled=True)
    dk, dv, dq = call(
        finish_body, 5, (shape((ROWS, 256)), shape((ROWS, 256)), shape((1, ROWS, 1024)))
    )(own, n1, n2, n3, dq)
    return jnp.transpose(dq, (1, 0, 2)), dk, dv


def solution(mesh):
    in_specs = (P("ctx", "kvh", None), P("ctx", "kvh"), P("ctx", "kvh"), P("ctx", "kvh", None), P())
    out_specs = (P("ctx", "kvh", None), P("ctx", "kvh"), P("ctx", "kvh"))
    return jax.shard_map(
        per_device, mesh=mesh, in_specs=in_specs, out_specs=out_specs, check_vma=False
    )
```

```python
import math

import jax
import jax.numpy as jnp
from jax import lax
from jax.experimental import pallas as pl
from jax.experimental.pallas import tpu as pltpu
from jax.sharding import PartitionSpec as P

HD = 128
ROWS = 256
BACK = 3
REPS = 4
HEADS = 2
SCALE = 1.0 / math.sqrt(HD)
RATE = SCALE / math.log(2.0)
NEAR = BACK * ROWS
UNITS = [(h, r) for h in range(HEADS) for r in range(REPS)]

NT = (((1,), (1,)), ((), ()))
NN = (((1,), (0,)), ((), ()))
TN = (((0,), (0,)), ((), ()))


def dot(a, b, dims):
    return lax.dot_general(a, b, dims, preferred_element_type=jnp.float32)


def sent(value, even, odd):
    length = lax.axis_size("ctx")
    moves = [(i, i + (odd if i % 2 else even)) for i in range(length)]
    return lax.ppermute(value, "ctx", [(i, j) for i, j in moves if 0 <= j < length])


def cols(h):
    return pl.ds(h * HD, HD)


def block_rows(b):
    return pl.ds(b * ROWS, ROWS)


def pack_body(len_ref, k_ref, v_ref, q_ref, g_ref, kv_ref, qg_ref, first_ref, len_buf, kv_buf, qg_buf, len_sem, sems):
    moves = [
        (ref.at[0, :, pl.ds(y * 256, 256)], qg_buf.at[y, a], qg_ref.at[y, a])
        for y in range(REPS)
        for a, ref in enumerate((q_ref, g_ref))
    ] + [(ref, kv_buf.at[a], kv_ref.at[a]) for a, ref in enumerate((k_ref, v_ref))]
    ins = [pltpu.make_async_copy(a, b, sems.at[0, n]) for n, (a, b, _) in enumerate(moves)]
    outs = [pltpu.make_async_copy(b, c, sems.at[1, n]) for n, (_, b, c) in enumerate(moves)]
    lens = pltpu.make_async_copy(len_ref, len_buf, len_sem)
    lens.start()
    for copy in ins:
        copy.start()
    lens.wait()
    first_ref[...] = doc_first(len_buf, lax.axis_index("ctx") * ROWS)
    for copy, after in zip(ins, outs):
        copy.wait()
        after.start()
    for copy in outs:
        copy.wait()


def doc_first(len_ref, origin):
    docs = len_ref.shape[1]
    at = lax.broadcasted_iota(jnp.int32, (docs, docs), 0)
    of = lax.broadcasted_iota(jnp.int32, (docs, docs), 1)
    ends = jnp.sum(jnp.where(of <= at, len_ref[...], 0), axis=1, keepdims=True)
    pos = origin + lax.broadcasted_iota(jnp.int32, (docs, ROWS), 1)
    return jnp.max(jnp.where(ends <= pos, ends, 0), axis=0, keepdims=True) - origin


def passed_back():
    odd = lax.rem(lax.axis_index("ctx"), 2)
    return 3 - 2 * odd, 1 + 2 * odd


def score(first, back, key, query):
    key_at = lax.broadcasted_iota(jnp.int32, (ROWS, ROWS), 0)
    allowed = key_at >= first + back * ROWS
    if isinstance(back, int) and back == 0:
        allowed = allowed & (key_at <= lax.broadcasted_iota(jnp.int32, (ROWS, ROWS), 1))
    return jnp.where(allowed, dot(key, query, NT), -1e30)


def near_body(first_ref, qg_ref, *refs):
    count = len(refs) - 5
    blocks = refs[:count]
    p_ref, d_ref, top_ref, total_ref, inner_ref = refs[count:]
    first = first_ref[...]
    backs = (2, passed_back()[0], 0)
    tops, totals, inners = {}, {}, {}

    def scores(u, n):
        h, r = UNITS[u]
        s = score(first, backs[n], blocks[n][0, :, cols(h)], qg_ref[r, 0, :, cols(h)])
        p_ref[u, block_rows(n), :] = s
        part = jnp.max(s, axis=0, keepdims=True)
        tops[u] = part if n == 0 else jnp.maximum(tops[u], part)

    def weigh(u, n):
        h, r = UNITS[u]
        p = jnp.exp2((p_ref[u, block_rows(n), :] - tops[u]) * RATE)
        d = dot(blocks[n][1, :, cols(h)], qg_ref[r, 1, :, cols(h)], NT)
        p_ref[u, block_rows(n), :] = p
        d_ref[u, block_rows(n), :] = d
        total, inner = jnp.sum(p, axis=0, keepdims=True), jnp.sum(p * d, axis=0, keepdims=True)
        totals[u] = total if n == 0 else totals[u] + total
        inners[u] = inner if n == 0 else inners[u] + inner
        if n == count - 1:
            top_ref[pl.ds(u, 1), :] = tops[u]
            total_ref[pl.ds(u, 1), :] = totals[u]
            inner_ref[pl.ds(u, 1), :] = inners[u]

    for step in range(len(UNITS) + 1):
        for n in range(count):
            if step < len(UNITS):
                scores(step, n)
            if step >= 1:
                weigh(step - 1, n)


def far_body(
    first_ref, top_ref, total_ref, inner_ref, p_ref, d_ref, qg_ref, *refs
):
    blocks = refs[:BACK + 1]
    outs = refs[BACK + 1:2 * BACK + 1]
    own_ref, dq_ref, s0_ref, d0_ref, w_ref, t_ref = refs[2 * BACK + 1:]
    near = p_ref.shape[1] // ROWS
    first = first_ref[...]
    backs = (passed_back()[1],)
    outs = outs[:near - 1] + (own_ref,) + outs[near - 1:]
    stats, norms = {}, {}

    def scores(u):
        h, r = UNITS[u]
        for b in range(near, BACK + 1):
            s = score(first, backs[b - near], blocks[b][0, :, cols(h)], qg_ref[r, 0, :, cols(h)])
            s0_ref[u, block_rows(b - near), :] = s
            top = jnp.max(s, axis=0, keepdims=True)
            stats[u] = top if b == near else jnp.maximum(top, stats[u])

    def weigh(u):
        h, r = UNITS[u]
        top = stats[u]
        far_total = far_inner = 0.0
        for b in range(near, BACK + 1):
            rows = block_rows(b - near)
            p = jnp.exp2((s0_ref[u, rows, :] - top) * RATE)
            d = dot(blocks[b][1, :, cols(h)], qg_ref[r, 1, :, cols(h)], NT)
            s0_ref[u, rows, :] = p
            d0_ref[u, rows, :] = d
            far_total = far_total + jnp.sum(p, axis=0, keepdims=True)
            far_inner = far_inner + jnp.sum(p * d, axis=0, keepdims=True)
        row = pl.ds(u, 1)
        whole = jnp.maximum(top, top_ref[row, :])
        far_part, near_part = jnp.exp2((top - whole) * RATE), jnp.exp2((top_ref[row, :] - whole) * RATE)
        total = near_part * total_ref[row, :] + far_part * far_total
        inner = near_part * inner_ref[row, :] + far_part * far_inner
        inverse = 1.0 / total
        norms[u] = (far_part * inverse, near_part * inverse, inner * inverse)

    def settle(u, b):
        h, r = UNITS[u]
        far_norm, near_norm, delta = norms[u]
        at = pl.ds(r * ROWS, ROWS)
        if b >= near:
            w, d = s0_ref[u, block_rows(b - near), :] * far_norm, d0_ref[u, block_rows(b - near), :]
        else:
            w, d = p_ref[u, block_rows(b), :] * near_norm, d_ref[u, block_rows(b), :]
        low, t = w.astype(jnp.bfloat16), (w * (d - delta)).astype(jnp.bfloat16)
        t_ref[h, block_rows(b), at] = t
        w_ref[h, block_rows(b), at] = low

    def query_grad(u):
        h, r = UNITS[u]
        keys = jnp.concatenate([block[0, :, cols(h)] for block in blocks], axis=0)
        dq = dot(keys, t_ref[h, :, pl.ds(r * ROWS, ROWS)], TN) * SCALE
        dq_ref[r, :, cols(h)] = dq.T.astype(jnp.bfloat16)

    def gather(h, b):
        queries = jnp.concatenate([qg_ref[r, 0, :, cols(h)] for r in range(REPS)], axis=0)
        grads = jnp.concatenate([qg_ref[r, 1, :, cols(h)] for r in range(REPS)], axis=0)
        dk = dot(t_ref[h, block_rows(b), :], queries, NN) * SCALE
        dv = dot(w_ref[h, block_rows(b), :], grads, NN)
        outs[b][0, :, cols(h)] = dk.astype(outs[b].dtype)
        outs[b][1, :, cols(h)] = dv.astype(outs[b].dtype)

    for step in range(len(UNITS) + 3):
        if step < len(UNITS):
            scores(step)
        if 0 <= step - 1 < len(UNITS):
            weigh(step - 1)
        if 0 <= step - 2 < len(UNITS):
            for b in range(BACK + 1):
                settle(step - 2, b)
        if 0 <= step - 3 < len(UNITS):
            query_grad(step - 3)
        if 0 <= step - 6 <= BACK:
            gather(0, step - 6)
    for b in range(BACK + 1):
        gather(1, b)


def add_body(a_ref, b_ref, c_ref):
    c_ref[...] = (a_ref[...].astype(jnp.float32) + b_ref[...].astype(jnp.float32)).astype(jnp.bfloat16)


def finish_body(own, n1, n2, dq_ref, k_ref, v_ref, q_ref):
    total = own[...] + (n1[...].astype(jnp.float32) + n2[...].astype(jnp.float32))
    k_ref[...] = total[0].astype(jnp.bfloat16)
    v_ref[...] = total[1].astype(jnp.bfloat16)
    for y in range(REPS):
        q_ref[0, :, pl.ds(y * 256, 256)] = dq_ref[y]


VM = pl.BlockSpec(memory_space=pltpu.VMEM)
ANY = pl.BlockSpec(memory_space=pl.ANY)


def call(body, n_in, out_shape, scratch=(), flops=0, bytes_=1 << 20, vmem=16 << 20, spec=VM, ospec=None):
    return pl.pallas_call(
        body,
        out_shape=out_shape,
        in_specs=[spec] * n_in,
        out_specs=ospec or jax.tree.map(lambda _: spec, out_shape),
        scratch_shapes=list(scratch),
        compiler_params=pltpu.CompilerParams(vmem_limit_bytes=vmem),
        cost_estimate=pl.CostEstimate(flops=flops, bytes_accessed=bytes_, transcendentals=0),
    )


def shape(dims, dtype=jnp.bfloat16):
    return jax.ShapeDtypeStruct(dims, dtype)


def per_device(queries, keys, values, out_grad, doc_lengths):
    q = jnp.transpose(queries, (1, 0, 2))
    g = jnp.transpose(out_grad, (1, 0, 2))
    block = (2, ROWS, 256)
    kv, qg, first = call(
        pack_body,
        5,
        (shape(block), shape((REPS, 2, ROWS, 256)), shape((1, ROWS), jnp.int32)),
        scratch=[
            pltpu.VMEM((1, doc_lengths.shape[0]), jnp.int32),
            pltpu.VMEM(block, jnp.bfloat16),
            pltpu.VMEM((REPS, 2, ROWS, 256), jnp.bfloat16),
            pltpu.SemaphoreType.DMA,
            pltpu.SemaphoreType.DMA((2, 10)),
        ],
        spec=ANY,
        ospec=(ANY, ANY, VM),
        vmem=4 << 20,
    )(*[pltpu.with_memory_space_constraint(x, pltpu.HBM) for x in (doc_lengths.reshape(1, -1), keys, values, q, g)])
    two = sent(kv, 2, 2)
    mixed = sent(kv, 1, 3)
    qg = lax.all_to_all(qg, "kvh", 0, 0, tiled=True)
    swapped = sent(two, 1, -1)
    units = len(UNITS)
    near, far = (two, mixed, kv), (swapped,)
    stat = shape((units, ROWS), jnp.float32)
    half = shape((units, len(near) * ROWS, ROWS), jnp.float32)
    p, d, top, total, inner = call(
        near_body, 2 + len(near), (half, half, stat, stat, stat), flops=1 << 30, vmem=4 << 20,
    )(first, qg, *near)
    p_two, p_mixed, p_swapped, own, dq = call(
        far_body,
        11,
        (shape(block),) * 3 + (shape(block, jnp.float32), shape((REPS, ROWS, 256))),
        scratch=(
            pltpu.VMEM((units, len(far) * ROWS, ROWS), jnp.float32),
            pltpu.VMEM((units, len(far) * ROWS, ROWS), jnp.float32),
            pltpu.VMEM((HEADS, 4 * ROWS, REPS * ROWS), jnp.bfloat16),
            pltpu.VMEM((HEADS, 4 * ROWS, REPS * ROWS), jnp.bfloat16),
        ),
        flops=1 << 30,
        vmem=16 << 20,
    )(first, top, total, inner, p, d, qg, *near, *far)
    from_swap = sent(p_swapped, 1, -1)
    from_mixed = sent(p_mixed, -3, -1)
    p_two = call(add_body, 2, shape(block), vmem=4 << 20)(p_two, from_swap)
    from_two = sent(p_two, -2, -2)
    dq = lax.all_to_all(dq, "kvh", 0, 0, tiled=True)
    dk, dv, dq = call(
        finish_body, 4, (shape((ROWS, 256)), shape((ROWS, 256)), shape((1, ROWS, 1024))), vmem=8 << 20,
    )(own, from_mixed, from_two, dq)
    return jnp.transpose(dq, (1, 0, 2)), dk, dv


def solution(mesh):
    in_specs = (P("ctx", "kvh", None), P("ctx", "kvh"), P("ctx", "kvh"), P("ctx", "kvh", None), P())
    out_specs = (P("ctx", "kvh", None), P("ctx", "kvh"), P("ctx", "kvh"))
    return jax.shard_map(
        per_device, mesh=mesh, in_specs=in_specs, out_specs=out_specs, check_vma=False
    )
```

```python
import math

import jax
import jax.numpy as jnp
from jax import lax
from jax.experimental import pallas as pl
from jax.experimental.pallas import tpu as pltpu
from jax.sharding import PartitionSpec as P

HD = 128
ROWS = 256
BACK = 3
REPS = 4
HEADS = 2
SCALE = 1.0 / math.sqrt(HD)
RATE = SCALE / math.log(2.0)
NEAR = BACK * ROWS
UNITS = [(h, r) for h in range(HEADS) for r in range(REPS)]

NT = (((1,), (1,)), ((), ()))
NN = (((1,), (0,)), ((), ()))
TN = (((0,), (0,)), ((), ()))


def dot(a, b, dims):
    return lax.dot_general(a, b, dims, preferred_element_type=jnp.float32)


def sent(value, even, odd):
    length = lax.axis_size("ctx")
    moves = [(i, i + (odd if i % 2 else even)) for i in range(length)]
    return lax.ppermute(value, "ctx", [(i, j) for i, j in moves if 0 <= j < length])


def cols(h):
    return pl.ds(h * HD, HD)


def block_rows(b):
    return pl.ds(b * ROWS, ROWS)


def pack_body(len_ref, k_ref, v_ref, q_ref, g_ref, kv_ref, qg_ref, first_ref, len_buf, len_sem, sems):
    moves = [
        (ref.at[0, :, pl.ds(y * 256, 256)], qg_ref.at[y, a])
        for y in range(REPS)
        for a, ref in enumerate((q_ref, g_ref))
    ] + [(ref, kv_ref.at[a]) for a, ref in enumerate((k_ref, v_ref))]
    lens = pltpu.make_async_copy(len_ref, len_buf, len_sem)
    lens.start()
    copies = [pltpu.make_async_copy(a, b, sems.at[n]) for n, (a, b) in enumerate(moves)]
    for copy in copies:
        copy.start()
    lens.wait()
    first_ref[...] = doc_first(len_buf, lax.axis_index("ctx") * ROWS)
    for copy in copies:
        copy.wait()


def doc_first(len_ref, origin):
    docs = len_ref.shape[1]
    at = lax.broadcasted_iota(jnp.int32, (docs, docs), 0)
    of = lax.broadcasted_iota(jnp.int32, (docs, docs), 1)
    ends = jnp.sum(jnp.where(of <= at, len_ref[...], 0), axis=1, keepdims=True)
    pos = origin + lax.broadcasted_iota(jnp.int32, (docs, ROWS), 1)
    return jnp.max(jnp.where(ends <= pos, ends, 0), axis=0, keepdims=True) - origin


def passed_back():
    odd = lax.rem(lax.axis_index("ctx"), 2)
    return 3 - 2 * odd, 1 + 2 * odd


def score(first, back, key, query):
    key_at = lax.broadcasted_iota(jnp.int32, (ROWS, ROWS), 0)
    allowed = key_at >= first + back * ROWS
    if isinstance(back, int) and back == 0:
        allowed = allowed & (key_at <= lax.broadcasted_iota(jnp.int32, (ROWS, ROWS), 1))
    return jnp.where(allowed, dot(key, query, NT), -1e30)


def near_body(first_ref, qg_ref, *refs):
    count = len(refs) - 5
    blocks = refs[:count]
    p_ref, d_ref, top_ref, total_ref, inner_ref = refs[count:]
    first = first_ref[...]
    backs = (2, passed_back()[0], 0)
    tops, totals, inners = {}, {}, {}

    def scores(u, n):
        h, r = UNITS[u]
        s = score(first, backs[n], blocks[n][0, :, cols(h)], qg_ref[r, 0, :, cols(h)])
        p_ref[u, block_rows(n), :] = s
        part = jnp.max(s, axis=0, keepdims=True)
        tops[u] = part if n == 0 else jnp.maximum(tops[u], part)

    def weigh(u, n):
        h, r = UNITS[u]
        p = jnp.exp2((p_ref[u, block_rows(n), :] - tops[u]) * RATE)
        d = dot(blocks[n][1, :, cols(h)], qg_ref[r, 1, :, cols(h)], NT)
        p_ref[u, block_rows(n), :] = p
        d_ref[u, block_rows(n), :] = d
        total, inner = jnp.sum(p, axis=0, keepdims=True), jnp.sum(p * d, axis=0, keepdims=True)
        totals[u] = total if n == 0 else totals[u] + total
        inners[u] = inner if n == 0 else inners[u] + inner
        if n == count - 1:
            top_ref[pl.ds(u, 1), :] = tops[u]
            total_ref[pl.ds(u, 1), :] = totals[u]
            inner_ref[pl.ds(u, 1), :] = inners[u]

    for step in range(len(UNITS) + 1):
        for n in range(count):
            if step < len(UNITS):
                scores(step, n)
            if step >= 1:
                weigh(step - 1, n)


def far_body(
    first_ref, top_ref, total_ref, inner_ref, p_ref, d_ref, qg_ref, *refs
):
    blocks = refs[:BACK + 1]
    outs = refs[BACK + 1:2 * BACK + 1]
    own_ref, dq_ref, s0_ref, d0_ref, w_ref, t_ref = refs[2 * BACK + 1:]
    near = p_ref.shape[1] // ROWS
    first = first_ref[...]
    backs = (passed_back()[1],)
    outs = outs[:near - 1] + (own_ref,) + outs[near - 1:]
    stats, norms = {}, {}

    def scores(u):
        h, r = UNITS[u]
        for b in range(near, BACK + 1):
            s = score(first, backs[b - near], blocks[b][0, :, cols(h)], qg_ref[r, 0, :, cols(h)])
            s0_ref[u, block_rows(b - near), :] = s
            top = jnp.max(s, axis=0, keepdims=True)
            stats[u] = top if b == near else jnp.maximum(top, stats[u])

    def weigh(u):
        h, r = UNITS[u]
        top = stats[u]
        far_total = far_inner = 0.0
        for b in range(near, BACK + 1):
            rows = block_rows(b - near)
            p = jnp.exp2((s0_ref[u, rows, :] - top) * RATE)
            d = dot(blocks[b][1, :, cols(h)], qg_ref[r, 1, :, cols(h)], NT)
            s0_ref[u, rows, :] = p
            d0_ref[u, rows, :] = d
            far_total = far_total + jnp.sum(p, axis=0, keepdims=True)
            far_inner = far_inner + jnp.sum(p * d, axis=0, keepdims=True)
        row = pl.ds(u, 1)
        whole = jnp.maximum(top, top_ref[row, :])
        far_part, near_part = jnp.exp2((top - whole) * RATE), jnp.exp2((top_ref[row, :] - whole) * RATE)
        total = near_part * total_ref[row, :] + far_part * far_total
        inner = near_part * inner_ref[row, :] + far_part * far_inner
        inverse = 1.0 / total
        norms[u] = (far_part * inverse, near_part * inverse, inner * inverse)

    def settle(u, b):
        h, r = UNITS[u]
        far_norm, near_norm, delta = norms[u]
        at = pl.ds(r * ROWS, ROWS)
        if b >= near:
            w, d = s0_ref[u, block_rows(b - near), :] * far_norm, d0_ref[u, block_rows(b - near), :]
        else:
            w, d = p_ref[u, block_rows(b), :] * near_norm, d_ref[u, block_rows(b), :]
        low, t = w.astype(jnp.bfloat16), (w * (d - delta)).astype(jnp.bfloat16)
        t_ref[h, block_rows(b), at] = t
        w_ref[h, block_rows(b), at] = low

    def query_grad(u):
        h, r = UNITS[u]
        keys = jnp.concatenate([block[0, :, cols(h)] for block in blocks], axis=0)
        dq = dot(keys, t_ref[h, :, pl.ds(r * ROWS, ROWS)], TN) * SCALE
        dq_ref[r, :, cols(h)] = dq.T.astype(jnp.bfloat16)

    def gather(h, b):
        queries = jnp.concatenate([qg_ref[r, 0, :, cols(h)] for r in range(REPS)], axis=0)
        grads = jnp.concatenate([qg_ref[r, 1, :, cols(h)] for r in range(REPS)], axis=0)
        dk = dot(t_ref[h, block_rows(b), :], queries, NN) * SCALE
        dv = dot(w_ref[h, block_rows(b), :], grads, NN)
        outs[b][0, :, cols(h)] = dk.astype(outs[b].dtype)
        outs[b][1, :, cols(h)] = dv.astype(outs[b].dtype)

    for step in range(len(UNITS) + 3):
        if step < len(UNITS):
            scores(step)
        if 0 <= step - 1 < len(UNITS):
            weigh(step - 1)
        if 0 <= step - 2 < len(UNITS):
            for b in range(BACK + 1):
                settle(step - 2, b)
        if 0 <= step - 3 < len(UNITS):
            query_grad(step - 3)
        if 0 <= step - 6 <= BACK:
            gather(0, step - 6)
    for b in range(BACK + 1):
        gather(1, b)


def add_body(a_ref, b_ref, c_ref):
    other = b_ref[1 - lax.rem(lax.axis_index("ctx"), 2)]
    c_ref[...] = (a_ref[...].astype(jnp.float32) + other.astype(jnp.float32)).astype(jnp.bfloat16)


def rest_body(own, n1, dq_ref, sum_ref, q_ref):
    sum_ref[...] = own[...] + n1[...].astype(jnp.float32)
    for y in range(REPS):
        q_ref[0, :, pl.ds(y * 256, 256)] = dq_ref[y]


def finish_body(sum_ref, n2, k_ref, v_ref):
    k_ref[...] = (sum_ref[0] + n2[0].astype(jnp.float32)).astype(jnp.bfloat16)
    v_ref[...] = (sum_ref[1] + n2[1].astype(jnp.float32)).astype(jnp.bfloat16)


VM = pl.BlockSpec(memory_space=pltpu.VMEM)
ANY = pl.BlockSpec(memory_space=pl.ANY)


def call(body, n_in, out_shape, scratch=(), flops=0, bytes_=1 << 20, vmem=16 << 20, spec=VM, ospec=None):
    return pl.pallas_call(
        body,
        out_shape=out_shape,
        in_specs=[spec] * n_in,
        out_specs=ospec or jax.tree.map(lambda _: spec, out_shape),
        scratch_shapes=list(scratch),
        compiler_params=pltpu.CompilerParams(vmem_limit_bytes=vmem),
        cost_estimate=pl.CostEstimate(flops=flops, bytes_accessed=bytes_, transcendentals=0),
    )


def shape(dims, dtype=jnp.bfloat16):
    return jax.ShapeDtypeStruct(dims, dtype)


def per_device(queries, keys, values, out_grad, doc_lengths):
    q = jnp.transpose(queries, (1, 0, 2))
    g = jnp.transpose(out_grad, (1, 0, 2))
    block = (2, ROWS, 256)
    kv, qg, first = call(
        pack_body,
        5,
        (shape(block), pltpu.VMEM((REPS, 2, ROWS, 256), jnp.bfloat16), shape((1, ROWS), jnp.int32)),
        scratch=[
            pltpu.VMEM((1, doc_lengths.shape[0]), jnp.int32),
            pltpu.SemaphoreType.DMA,
            pltpu.SemaphoreType.DMA((10,)),
        ],
        spec=ANY,
        ospec=(VM, VM, VM),
        vmem=4 << 20,
    )(*[pltpu.with_memory_space_constraint(x, pltpu.HBM) for x in (doc_lengths.reshape(1, -1), keys, values, q, g)])
    two = sent(kv, 2, 2)
    mixed = sent(kv, 1, 3)
    qg = lax.all_to_all(qg, "kvh", 0, 0, tiled=True)
    swapped = sent(two, 1, -1)
    units = len(UNITS)
    near, far = (two, mixed, kv), (swapped,)
    stat = shape((units, ROWS), jnp.float32)
    half = shape((units, len(near) * ROWS, ROWS), jnp.float32)
    p, d, top, total, inner = call(
        near_body, 2 + len(near), (half, half, stat, stat, stat), flops=1 << 30, vmem=4 << 20,
    )(first, qg, *near)
    p_two, p_mixed, p_swapped, own, dq = call(
        far_body,
        11,
        (shape(block),) * 3 + (shape(block, jnp.float32), pltpu.VMEM((REPS, ROWS, 256), jnp.bfloat16)),
        scratch=(
            pltpu.VMEM((units, len(far) * ROWS, ROWS), jnp.float32),
            pltpu.VMEM((units, len(far) * ROWS, ROWS), jnp.float32),
            pltpu.VMEM((HEADS, 4 * ROWS, REPS * ROWS), jnp.bfloat16),
            pltpu.VMEM((HEADS, 4 * ROWS, REPS * ROWS), jnp.bfloat16),
        ),
        flops=1 << 30,
        vmem=16 << 20,
    )(first, top, total, inner, p, d, qg, *near, *far)
    pairs = [[i, i + 1] for i in range(0, lax.axis_size("ctx"), 2)]
    from_swap = lax.all_gather(p_swapped, "ctx", axis_index_groups=pairs)
    from_mixed = sent(p_mixed, -3, -1)
    p_two = call(add_body, 2, shape(block), vmem=4 << 20)(p_two, from_swap)
    from_two = sent(p_two, -2, -2)
    dq = lax.all_to_all(dq, "kvh", 0, 0, tiled=True)
    own, dq = call(
        rest_body, 3, (shape(block, jnp.float32), shape((1, ROWS, 1024))), vmem=4 << 20,
    )(own, from_mixed, dq)
    dk, dv = call(finish_body, 2, (shape((ROWS, 256)), shape((ROWS, 256))), vmem=4 << 20)(own, from_two)
    return jnp.transpose(dq, (1, 0, 2)), dk, dv


def solution(mesh):
    in_specs = (P("ctx", "kvh", None), P("ctx", "kvh"), P("ctx", "kvh"), P("ctx", "kvh", None), P())
    out_specs = (P("ctx", "kvh", None), P("ctx", "kvh"), P("ctx", "kvh"))
    return jax.shard_map(
        per_device, mesh=mesh, in_specs=in_specs, out_specs=out_specs, check_vma=False
    )
```

```python
import math

import jax
import jax.numpy as jnp
from jax import lax
from jax.experimental import pallas as pl
from jax.experimental.pallas import tpu as pltpu
from jax.sharding import PartitionSpec as P

HD = 128
ROWS = 256
BACK = 3
REPS = 4
HEADS = 2
SCALE = 1.0 / math.sqrt(HD)
RATE = SCALE / math.log(2.0)
NEAR = BACK * ROWS
UNITS = [(h, r) for h in range(HEADS) for r in range(REPS)]

NT = (((1,), (1,)), ((), ()))
NN = (((1,), (0,)), ((), ()))
TN = (((0,), (0,)), ((), ()))


def dot(a, b, dims):
    return lax.dot_general(a, b, dims, preferred_element_type=jnp.float32)


def sent(value, even, odd):
    length = lax.axis_size("ctx")
    moves = [(i, i + (odd if i % 2 else even)) for i in range(length)]
    return lax.ppermute(value, "ctx", [(i, j) for i, j in moves if 0 <= j < length])


def cols(h):
    return pl.ds(h * HD, HD)


def block_rows(b):
    return pl.ds(b * ROWS, ROWS)


def pack_body(len_ref, k_ref, v_ref, q_ref, g_ref, kv_ref, qg_ref, first_ref, len_buf, len_sem, sems):
    moves = [
        (ref.at[0, :, pl.ds(y * 256, 256)], qg_ref.at[y, a])
        for y in range(REPS)
        for a, ref in enumerate((q_ref, g_ref))
    ] + [(ref, kv_ref.at[a]) for a, ref in enumerate((k_ref, v_ref))]
    lens = pltpu.make_async_copy(len_ref, len_buf, len_sem)
    lens.start()
    copies = [pltpu.make_async_copy(a, b, sems.at[n]) for n, (a, b) in enumerate(moves)]
    for copy in copies:
        copy.start()
    lens.wait()
    first_ref[...] = doc_first(len_buf, lax.axis_index("ctx") * ROWS)
    for copy in copies:
        copy.wait()


def doc_first(len_ref, origin):
    docs = len_ref.shape[1]
    at = lax.broadcasted_iota(jnp.int32, (docs, docs), 0)
    of = lax.broadcasted_iota(jnp.int32, (docs, docs), 1)
    ends = jnp.sum(jnp.where(of <= at, len_ref[...], 0), axis=1, keepdims=True)
    pos = origin + lax.broadcasted_iota(jnp.int32, (docs, ROWS), 1)
    return jnp.max(jnp.where(ends <= pos, ends, 0), axis=0, keepdims=True) - origin


def passed_back():
    odd = lax.rem(lax.axis_index("ctx"), 2)
    return 3 - 2 * odd, 1 + 2 * odd


def score(first, back, key, query):
    key_at = lax.broadcasted_iota(jnp.int32, (ROWS, ROWS), 0)
    allowed = key_at >= first + back * ROWS
    if isinstance(back, int) and back == 0:
        allowed = allowed & (key_at <= lax.broadcasted_iota(jnp.int32, (ROWS, ROWS), 1))
    return jnp.where(allowed, dot(key, query, NT), -1e30)


def near_body(first_ref, qg_ref, *refs):
    count = len(refs) - 5
    blocks = refs[:count]
    p_ref, d_ref, top_ref, total_ref, inner_ref = refs[count:]
    first = first_ref[...]
    backs = (2, passed_back()[0], 0)
    tops, totals, inners = {}, {}, {}

    def scores(u, n):
        h, r = UNITS[u]
        s = score(first, backs[n], blocks[n][0, :, cols(h)], qg_ref[r, 0, :, cols(h)])
        p_ref[u, block_rows(n), :] = s
        part = jnp.max(s, axis=0, keepdims=True)
        tops[u] = part if n == 0 else jnp.maximum(tops[u], part)

    def weigh(u, n):
        h, r = UNITS[u]
        p = jnp.exp2((p_ref[u, block_rows(n), :] - tops[u]) * RATE)
        d = dot(blocks[n][1, :, cols(h)], qg_ref[r, 1, :, cols(h)], NT)
        p_ref[u, block_rows(n), :] = p
        d_ref[u, block_rows(n), :] = d
        total, inner = jnp.sum(p, axis=0, keepdims=True), jnp.sum(p * d, axis=0, keepdims=True)
        totals[u] = total if n == 0 else totals[u] + total
        inners[u] = inner if n == 0 else inners[u] + inner
        if n == count - 1:
            top_ref[pl.ds(u, 1), :] = tops[u]
            total_ref[pl.ds(u, 1), :] = totals[u]
            inner_ref[pl.ds(u, 1), :] = inners[u]

    for step in range(len(UNITS) + 1):
        for n in range(count):
            if step < len(UNITS):
                scores(step, n)
            if step >= 1:
                weigh(step - 1, n)


def far_body(
    first_ref, top_ref, total_ref, inner_ref, p_ref, d_ref, qg_ref, *refs
):
    blocks = refs[:BACK + 1]
    outs = refs[BACK + 1:2 * BACK + 1]
    own_ref, dq_ref, s0_ref, d0_ref, w_ref, t_ref = refs[2 * BACK + 1:]
    near = p_ref.shape[1] // ROWS
    first = first_ref[...]
    backs = (passed_back()[1],)
    outs = outs[:near - 1] + (own_ref,) + outs[near - 1:]
    stats, norms = {}, {}

    def scores(u):
        h, r = UNITS[u]
        for b in range(near, BACK + 1):
            s = score(first, backs[b - near], blocks[b][0, :, cols(h)], qg_ref[r, 0, :, cols(h)])
            s0_ref[u, block_rows(b - near), :] = s
            top = jnp.max(s, axis=0, keepdims=True)
            stats[u] = top if b == near else jnp.maximum(top, stats[u])

    def weigh(u):
        h, r = UNITS[u]
        top = stats[u]
        far_total = far_inner = 0.0
        for b in range(near, BACK + 1):
            rows = block_rows(b - near)
            p = jnp.exp2((s0_ref[u, rows, :] - top) * RATE)
            d = dot(blocks[b][1, :, cols(h)], qg_ref[r, 1, :, cols(h)], NT)
            s0_ref[u, rows, :] = p
            d0_ref[u, rows, :] = d
            far_total = far_total + jnp.sum(p, axis=0, keepdims=True)
            far_inner = far_inner + jnp.sum(p * d, axis=0, keepdims=True)
        row = pl.ds(u, 1)
        whole = jnp.maximum(top, top_ref[row, :])
        far_part, near_part = jnp.exp2((top - whole) * RATE), jnp.exp2((top_ref[row, :] - whole) * RATE)
        total = near_part * total_ref[row, :] + far_part * far_total
        inner = near_part * inner_ref[row, :] + far_part * far_inner
        inverse = 1.0 / total
        norms[u] = (far_part * inverse, near_part * inverse, inner * inverse)

    def settle(u, b):
        h, r = UNITS[u]
        far_norm, near_norm, delta = norms[u]
        at = pl.ds(r * ROWS, ROWS)
        if b >= near:
            w, d = s0_ref[u, block_rows(b - near), :] * far_norm, d0_ref[u, block_rows(b - near), :]
        else:
            w, d = p_ref[u, block_rows(b), :] * near_norm, d_ref[u, block_rows(b), :]
        low, t = w.astype(jnp.bfloat16), (w * (d - delta)).astype(jnp.bfloat16)
        t_ref[h, block_rows(b), at] = t
        w_ref[h, block_rows(b), at] = low

    def query_grad(u):
        h, r = UNITS[u]
        keys = jnp.concatenate([block[0, :, cols(h)] for block in blocks], axis=0)
        dq = dot(keys, t_ref[h, :, pl.ds(r * ROWS, ROWS)], TN) * SCALE
        dq_ref[r, :, cols(h)] = dq.T.astype(jnp.bfloat16)

    def gather(h, b):
        queries = jnp.concatenate([qg_ref[r, 0, :, cols(h)] for r in range(REPS)], axis=0)
        grads = jnp.concatenate([qg_ref[r, 1, :, cols(h)] for r in range(REPS)], axis=0)
        if b == near - 1:
            half = ROWS // 2
            low_rows = pl.ds(b * ROWS, half)
            late = [pl.ds(r * ROWS + half, half) for r in range(REPS)]
            high = pl.ds(b * ROWS + half, half)

            def both(ref, other, a):
                cut = jnp.concatenate([ref[h, high, at] for at in late], axis=1)
                rows = jnp.concatenate([qg_ref[r, a, pl.ds(half, half), cols(h)] for r in range(REPS)], axis=0)
                return jnp.concatenate([dot(ref[h, low_rows, :], other, NN), dot(cut, rows, NN)], axis=0)

            dk, dv = both(t_ref, queries, 0) * SCALE, both(w_ref, grads, 1)
        else:
            dk = dot(t_ref[h, block_rows(b), :], queries, NN) * SCALE
            dv = dot(w_ref[h, block_rows(b), :], grads, NN)
        outs[b][0, :, cols(h)] = dk.astype(outs[b].dtype)
        outs[b][1, :, cols(h)] = dv.astype(outs[b].dtype)

    for step in range(len(UNITS) + 3):
        if step < len(UNITS):
            scores(step)
        if 0 <= step - 1 < len(UNITS):
            weigh(step - 1)
        if 0 <= step - 2 < len(UNITS):
            for b in range(BACK + 1):
                settle(step - 2, b)
        if 0 <= step - 3 < len(UNITS):
            query_grad(step - 3)
        if 0 <= step - 6 <= BACK:
            gather(0, step - 6)
    for b in range(BACK + 1):
        gather(1, b)


def add_body(a_ref, b_ref, c_ref):
    other = b_ref[1 - lax.rem(lax.axis_index("ctx"), 2)]
    c_ref[...] = (a_ref[...].astype(jnp.float32) + other.astype(jnp.float32)).astype(jnp.bfloat16)


def rest_body(own, n1, dq_ref, sum_ref, q_ref):
    sum_ref[...] = own[...] + n1[...].astype(jnp.float32)
    for y in range(REPS):
        q_ref[0, :, pl.ds(y * 256, 256)] = dq_ref[y]


def finish_body(sum_ref, n2, k_ref, v_ref):
    k_ref[...] = (sum_ref[0] + n2[0].astype(jnp.float32)).astype(jnp.bfloat16)
    v_ref[...] = (sum_ref[1] + n2[1].astype(jnp.float32)).astype(jnp.bfloat16)


VM = pl.BlockSpec(memory_space=pltpu.VMEM)
ANY = pl.BlockSpec(memory_space=pl.ANY)


def call(body, n_in, out_shape, scratch=(), flops=0, bytes_=1 << 20, vmem=16 << 20, spec=VM, ospec=None):
    return pl.pallas_call(
        body,
        out_shape=out_shape,
        in_specs=[spec] * n_in,
        out_specs=ospec or jax.tree.map(lambda _: spec, out_shape),
        scratch_shapes=list(scratch),
        compiler_params=pltpu.CompilerParams(vmem_limit_bytes=vmem),
        cost_estimate=pl.CostEstimate(flops=flops, bytes_accessed=bytes_, transcendentals=0),
    )


def shape(dims, dtype=jnp.bfloat16):
    return jax.ShapeDtypeStruct(dims, dtype)


def per_device(queries, keys, values, out_grad, doc_lengths):
    q = jnp.transpose(queries, (1, 0, 2))
    g = jnp.transpose(out_grad, (1, 0, 2))
    block = (2, ROWS, 256)
    kv, qg, first = call(
        pack_body,
        5,
        (shape(block), pltpu.VMEM((REPS, 2, ROWS, 256), jnp.bfloat16), shape((1, ROWS), jnp.int32)),
        scratch=[
            pltpu.VMEM((1, doc_lengths.shape[0]), jnp.int32),
            pltpu.SemaphoreType.DMA,
            pltpu.SemaphoreType.DMA((10,)),
        ],
        spec=ANY,
        ospec=(VM, VM, VM),
        vmem=4 << 20,
    )(*[pltpu.with_memory_space_constraint(x, pltpu.HBM) for x in (doc_lengths.reshape(1, -1), keys, values, q, g)])
    two = sent(kv, 2, 2)
    mixed = sent(kv, 1, 3)
    qg = lax.all_to_all(qg, "kvh", 0, 0, tiled=True)
    swapped = sent(two, 1, -1)
    units = len(UNITS)
    near, far = (two, mixed, kv), (swapped,)
    stat = shape((units, ROWS), jnp.float32)
    half = shape((units, len(near) * ROWS, ROWS), jnp.float32)
    p, d, top, total, inner = call(
        near_body, 2 + len(near), (half, half, stat, stat, stat), flops=1 << 30, vmem=4 << 20,
    )(first, qg, *near)
    p_two, p_mixed, p_swapped, own, dq = call(
        far_body,
        11,
        (shape(block),) * 3 + (shape(block, jnp.float32), pltpu.VMEM((REPS, ROWS, 256), jnp.bfloat16)),
        scratch=(
            pltpu.VMEM((units, len(far) * ROWS, ROWS), jnp.float32),
            pltpu.VMEM((units, len(far) * ROWS, ROWS), jnp.float32),
            pltpu.VMEM((HEADS, 4 * ROWS, REPS * ROWS), jnp.bfloat16),
            pltpu.VMEM((HEADS, 4 * ROWS, REPS * ROWS), jnp.bfloat16),
        ),
        flops=1 << 30,
        vmem=16 << 20,
    )(first, top, total, inner, p, d, qg, *near, *far)
    pairs = [[i, i + 1] for i in range(0, lax.axis_size("ctx"), 2)]
    from_swap = lax.all_gather(p_swapped, "ctx", axis_index_groups=pairs)
    from_mixed = sent(p_mixed, -3, -1)
    p_two = call(add_body, 2, shape(block), vmem=4 << 20)(p_two, from_swap)
    from_two = sent(p_two, -2, -2)
    dq = lax.all_to_all(dq, "kvh", 0, 0, tiled=True)
    own, dq = call(
        rest_body, 3, (shape(block, jnp.float32), shape((1, ROWS, 1024))), vmem=4 << 20,
    )(own, from_mixed, dq)
    dk, dv = call(finish_body, 2, (shape((ROWS, 256)), shape((ROWS, 256))), vmem=4 << 20)(own, from_two)
    return jnp.transpose(dq, (1, 0, 2)), dk, dv


def solution(mesh):
    in_specs = (P("ctx", "kvh", None), P("ctx", "kvh"), P("ctx", "kvh"), P("ctx", "kvh", None), P())
    out_specs = (P("ctx", "kvh", None), P("ctx", "kvh"), P("ctx", "kvh"))
    return jax.shard_map(
        per_device, mesh=mesh, in_specs=in_specs, out_specs=out_specs, check_vma=False
    )
```
